32 devices in a mesh: row: 4 (over y, x), col: 8 (over z, core).
Axes of the slice: x: 2, y: 2, z: 4, core: 2. Of those that a mesh axis runs over, the one named last changes fastest.
Arguments:
- depth: float32 [1024, 4096], P('row', 'col'), may hold values from 0.5 to 3
- bed: float32 [1024, 4096], P('row', 'col'), may hold values from -1 to 1
- mass: float32 [1024, 4096], P('row', 'col'), may hold values from 0.2 to 2
- conduct: float32 [1024, 4096], P('row', 'col'), may hold values from 0.02 to 0.2
- settle: float32 [1024, 4096], P('row', 'col'), may hold values from 0.02 to 0.5
- wet: int32 [1024, 4096], P('row', 'col'), may hold values 0 or 1
- link_block: int32 [16384], P(('row', 'col')), may hold values from 0 to 1023
- link_owner: int32 [16384, 1], P(('row', 'col')), may hold values from 0 to 31; in each aligned block of 512 rows (0 to 511, 512 to 1023, ...) at most 32 rows name the same one
- link_reach: int32 [16384], P(('row', 'col')), may hold values from 0 to 15
- link_coef: float32 [16384], P(('row', 'col')), may hold values from 0.05 to 0.5
- chan_phase: float32 [512, 128], P(('row', 'col')), may hold values from -0.5 to 2
- chan_conc: float32 [512, 128], P(('row', 'col')), may hold values from 0.1 to 1
- chan_area: float32 [512, 128], P(('row', 'col')), may hold values from 2 to 20
Outputs:
- depth_out: float32 [1024, 4096], P('row', 'col')
- mass_out: float32 [1024, 4096], P('row', 'col')
- phase_out: float32 [512, 128], P(('row', 'col'))
- conc_out: float32 [512, 128], P(('row', 'col'))
The draws below stay inside these ranges and needn't reach their ends.
Inputs may be any that keep to these rules, and one draw needn't show every extreme that they name: `link_block`: block index within a tile. `link_owner`: among the 512 links of one tile, at most 32 name the same owner.
All inputs are finite; a program needn't handle non-finite values. No bound on the sum of `wet` on one device may be relied on, other than what follows from the above.
Results may differ from the reference program's by a relative error of at most 0.00005.
Values sent between devices are 32-bit elements; how exact they have to be, the bound alone decides.
A program may use at most 64 MiB of HBM per device.

```python
import math
import jax
import jax.numpy as jnp
import numpy as np

TILE_Y = 256
TILE_X = 512
LINKS_DEV = 512
REACH_DEV = 16
SECTIONS = 128
CAP = 32
NY = 1024
NX = 4096
LINKS = 16384
REACHES = 512
N_COL = 8
DEVICES = 32


def set_ends(values, rng, smallest, largest):
    place = [jax.random.randint(jax.random.fold_in(rng, axis), (), 0, length) for axis, length in enumerate(values.shape)]
    widest = values.shape.index(max(values.shape))
    neighbour = place[:widest] + [(place[widest] + 1) % values.shape[widest]] + place[widest + 1:]
    return values.at[tuple(place)].set(smallest).at[tuple(neighbour)].set(largest)


def block_levels(own_key, shape, cuts, smallest, top_value):
    loudness = 1.0
    for position, parts in cuts:
        heights = jax.random.uniform(jax.random.fold_in(jax.random.fold_in(own_key, 6), position), (parts,), jnp.float32, smallest / len(cuts), top_value / len(cuts))
        loudness = loudness * jnp.repeat(jnp.exp(heights), shape[position] // parts).reshape((-1,) + (1,) * (len(shape) - 1 - position))
    return loudness


def assign_block(rng, own, number, rows, amount, top, bound, lean):
    order = jax.random.permutation(rng, amount)
    packed, ordinary = shares(amount, rows * top, bound, lean, True), shares(amount, rows * top, bound, lean, False)
    places = jnp.arange(amount)

    def named(lengths, offset_by):
        used = int((lengths > 0).sum())
        fixed = max(1, used // 4)
        moved = fixed + (places - fixed + offset_by * (used - fixed)) % max(1, amount - fixed)
        return jnp.zeros((amount,), jnp.int32).at[order[jnp.where(places < fixed, places, moved)]].set(jnp.asarray(lengths, jnp.int32))

    lengths = jnp.where(number % 4 == 0, named(packed, number // 4), named(ordinary, number - number // 4 - 1))
    mixed = jax.random.permutation(jax.random.fold_in(own, 3), amount)
    donor, sink = mixed[0:amount // 2 * 2:2], mixed[1:amount // 2 * 2:2]
    room = jnp.minimum(lengths[donor] - 1, bound - lengths[sink]) // 2
    room = jnp.where((donor == order[0]) | (sink == order[0]) | (lengths[sink] == 0), 0, jnp.maximum(room, 0))
    moved = jax.random.randint(jax.random.fold_in(own, 4), (amount // 2,), 0, 1 << 20) % (room + 1)
    lengths = lengths.at[donor].add(-moved).at[sink].add(moved)
    labels = jnp.searchsorted(jnp.cumsum(lengths), jnp.arange(rows * top), side="right").astype(jnp.int32)
    grid = labels.reshape(top, rows).T
    grid = grid[jax.random.permutation(jax.random.fold_in(own, 1), rows)]
    offset_by = jax.random.randint(jax.random.fold_in(own, 2), (rows, 1), 0, top)
    return jnp.take_along_axis(grid, (jnp.arange(top)[None, :] + offset_by) % top, axis=1)


def shares(amount, total, most, lean, full):
    loads = [(1 << 20) // math.isqrt(grade ** lean) + 1 for grade in range(1, amount + 1)]
    largest = most if full else min(most, max(-(-total // amount), total * loads[0] // sum(loads)))
    least = 1 if total - largest >= amount - 1 else 0
    counts, rest = [largest] + [least] * (amount - 1), total - largest - least * (amount - 1)
    while rest > 0:
        candidates = [i for i in range(1, amount) if counts[i] < largest] or [i for i in range(1, amount) if counts[i] < most]
        pool, budget = sum([loads[i] for i in candidates]), rest
        for i in candidates:
            extra = min(most - counts[i], max(1, budget * loads[i] // pool), rest)
            counts[i] = counts[i] + extra
            rest = rest - extra
    return np.array(counts)


def setup_inputs(seed: int = 0) -> dict:
    splits = jax.random.split(jax.random.key(seed), 14)
    depth = jnp.clip(0.5 + 2.5 * jax.random.uniform(splits[0], (NY, NX), jnp.float32) ** block_levels(splits[0], (NY, NX), ((0, 4), (1, 8)), -0.2, 0.2), 0.5, 3.0)
    bed = jnp.clip(jax.random.uniform(splits[1], (NY, NX), jnp.float32, -1.0, 1.0) * block_levels(splits[1], (NY, NX), ((0, 4), (1, 8)), -0.4, 0.0), -1.0, 1.0)
    mass = jnp.clip(0.2 + 1.8 * jax.random.uniform(splits[2], (NY, NX), jnp.float32) ** block_levels(splits[2], (NY, NX), ((0, 4), (1, 8)), -0.2, 0.2), 0.2, 2.0)
    conduct = jnp.clip(jnp.exp(math.log(0.2) - 2.3025851 * jax.random.uniform(splits[3], (NY, NX), jnp.float32) ** block_levels(splits[3], (NY, NX), ((0, 4), (1, 8)), -0.2, 0.2)), 0.02, 0.2)
    settle = jnp.clip(jnp.exp(math.log(0.5) - 3.218876 * jax.random.uniform(splits[4], (NY, NX), jnp.float32) ** block_levels(splits[4], (NY, NX), ((0, 4), (1, 8)), -0.2, 0.2)), 0.02, 0.5)
    wet = set_ends((jax.random.randint(splits[5], (NY, NX), 0, 4) < 3).astype(jnp.int32), jax.random.fold_in(splits[5], 1), 0, 1)
    link_block = set_ends(jax.random.randint(splits[6], (LINKS,), 0, TILE_Y * TILE_X // 128), jax.random.fold_in(splits[6], 1), 0, (TILE_Y * TILE_X // 128) - 1).astype(jnp.int32)
    link_owner_keys = jax.random.split(jax.random.fold_in(splits[7], 1), LINKS // LINKS_DEV)
    link_owner_turns = jax.random.permutation(jax.random.fold_in(splits[7], 3), LINKS // LINKS_DEV)
    link_owner = jax.vmap(lambda own, number: assign_block(jax.random.fold_in(splits[7], 2), own, number, LINKS_DEV, DEVICES, 1, CAP, 2))(link_owner_keys, link_owner_turns).reshape((LINKS, 1))
    link_reach = set_ends(jax.random.randint(splits[8], (LINKS,), 0, REACH_DEV), jax.random.fold_in(splits[8], 1), 0, REACH_DEV - 1).astype(jnp.int32)
    link_coef = jnp.clip(jnp.exp(math.log(0.5) - 2.3025851 * jax.random.uniform(splits[9], (LINKS,), jnp.float32) ** block_levels(splits[9], (LINKS,), ((0, 32),), -0.2, 0.2)), 0.05, 0.5)
    chan_phase = jnp.clip(-0.5 + 2.5 * jax.random.uniform(splits[10], (REACHES, SECTIONS), jnp.float32) ** block_levels(splits[10], (REACHES, SECTIONS), ((0, 32),), -0.2, 0.2), -0.5, 2.0)
    chan_conc = jnp.clip(0.1 + 0.9 * jax.random.uniform(splits[11], (REACHES, SECTIONS), jnp.float32) ** block_levels(splits[11], (REACHES, SECTIONS), ((0, 32),), -0.2, 0.2), 0.1, 1.0)
    chan_area = jnp.clip(jnp.exp(math.log(20.0) - 2.3025851 * jax.random.uniform(splits[12], (REACHES, SECTIONS), jnp.float32) ** block_levels(splits[12], (REACHES, SECTIONS), ((0, 32),), -0.2, 0.2)), 2.0, 20.0)
    return dict(depth=depth, bed=bed, mass=mass, conduct=conduct, settle=settle, wet=wet, link_block=link_block, link_owner=link_owner, link_reach=link_reach, link_coef=link_coef, chan_phase=chan_phase, chan_conc=chan_conc, chan_area=chan_area)


def shifted(padded, step_y, step_x, size_y, size_x):
    return padded[1 + step_y:1 + step_y + size_y, 1 + step_x:1 + step_x + size_x]


def smooth_reach(values):
    left = jnp.concatenate([values[:, :1], values[:, :-1]], axis=1)
    right = jnp.concatenate([values[:, 1:], values[:, -1:]], axis=1)
    return values + 0.25 * (left - 2.0 * values + right)


def reference(depth, bed, mass, conduct, settle, wet, link_block, link_owner, link_reach, link_coef, chan_phase, chan_conc, chan_area):
    size_y, size_x = depth.shape
    surface = depth + bed
    opened = wet.astype(jnp.float32)
    pad_surf = jnp.pad(surface, 1)
    pad_mass = jnp.pad(mass, 1)
    pad_cond = jnp.pad(conduct, 1)
    pad_open = jnp.pad(opened, 1)
    water_gain = jnp.zeros_like(depth)
    mass_gain = jnp.zeros_like(depth)
    for step_y, step_x in ((1, 0), (-1, 0), (0, 1), (0, -1)):
        coeff = 0.5 * (conduct + shifted(pad_cond, step_y, step_x, size_y, size_x)) * opened * shifted(pad_open, step_y, step_x, size_y, size_x)
        water_gain = water_gain + coeff * (shifted(pad_surf, step_y, step_x, size_y, size_x) - surface)
        mass_gain = mass_gain + coeff * (shifted(pad_mass, step_y, step_x, size_y, size_x) - mass)
    depth1 = depth + water_gain
    mass1 = (mass + mass_gain) * jnp.exp(-settle)
    surface1 = depth1 + bed
    link_ids = jnp.arange(LINKS, dtype=jnp.int32)
    tile_ids = link_ids // LINKS_DEV
    tile_row = tile_ids // N_COL
    tile_col = tile_ids % N_COL
    per_row = TILE_X // 128
    cell_y = tile_row * TILE_Y + link_block // per_row
    cell_x0 = tile_col * TILE_X + (link_block % per_row) * 128
    cell_xs = cell_x0[:, None] + jnp.arange(128, dtype=jnp.int32)[None, :]
    cell_ys = jnp.broadcast_to(cell_y[:, None], cell_xs.shape)
    weight = link_coef[:, None] * opened[cell_ys, cell_xs]
    surf_rows = surface1[cell_ys, cell_xs]
    mass_rows = mass1[cell_ys, cell_xs]
    reach_ids = (link_owner[:, 0] * REACH_DEV + link_reach).astype(jnp.int32)
    inflow = jax.ops.segment_sum(weight * surf_rows, reach_ids, num_segments=REACHES)
    wet_sum = jax.ops.segment_sum(weight, reach_ids, num_segments=REACHES)
    sediment = jax.ops.segment_sum(weight * mass_rows, reach_ids, num_segments=REACHES)
    phase_new = (chan_area * chan_phase + inflow) / (chan_area + wet_sum)
    conc_new = (chan_area * chan_conc + sediment) / (chan_area + wet_sum)
    phase_out = smooth_reach(phase_new)
    conc_out = smooth_reach(conc_new)
    depth_out = depth1.at[cell_ys, cell_xs].add(0.5 * weight * (phase_out[reach_ids] - surf_rows))
    mass_out = mass1.at[cell_ys, cell_xs].add(0.5 * weight * (conc_out[reach_ids] - mass_rows))
    return depth_out, mass_out, phase_out, conc_out
```

```python
import functools

import jax
import jax.numpy as jnp
from jax import lax
from jax.experimental import pallas as pl
from jax.experimental.pallas import tpu as pltpu
from jax.sharding import PartitionSpec as P

MESH = pl.DeviceIdType.MESH
F32 = jnp.float32
BF16 = jnp.bfloat16
SEC = 128
BASE = 8
CHUNK = 16


def split(x):
    hi = x.astype(BF16)
    return hi, (x - hi.astype(F32)).astype(BF16)


def dot_nt(a, b):
    return lax.dot_general(a, b, (((1,), (1,)), ((), ())), preferred_element_type=F32)


def dot_nn(a, b):
    return jnp.dot(a, b, preferred_element_type=F32)


def smooth(v):
    lane = lax.broadcasted_iota(jnp.int32, v.shape, 1)
    left = jnp.where(lane == 0, v, pltpu.roll(v, 1, 1))
    right = jnp.where(lane == SEC - 1, v, pltpu.roll(v, SEC - 1, 1))
    return v + 0.25 * (left - 2.0 * v + right)


def kernel(
    n_row,
    n_col,
    depth_h,
    bed_h,
    mass_h,
    conduct_h,
    settle_h,
    wet_h,
    block_ref,
    reach_ref,
    coef_ref,
    phase_ref,
    conc_ref,
    area_ref,
    depth_out,
    mass_out,
    phase_out,
    conc_out,
    depth_v,
    bed_v,
    cond_v,
    settle_v,
    wet_v,
    s_pad,
    m_pad,
    c_pad,
    o_pad,
    d1,
    m1,
    s1,
    dcat,
    hot_l,
    hot_b,
    mat_hi,
    mat_lo,
    mt_hi,
    mt_lo,
    csum,
    part,
    r_core,
    q_row,
    r_row,
    s_z,
    r_z,
    table,
    row_send,
    row_recv,
    col_send,
    col_recv,
    in_sem,
    out_sem,
    halo_s,
    halo_r,
    core_s,
    core_r,
    row_s,
    row_r,
    z_s,
    z_r,
    gz_s,
    gz_r,
    gr_s,
    gr_r,
    gc_s,
    gc_r,
):
    rows, cols = depth_v.shape
    n_z = n_col // 2
    half = part.shape[2]
    nblk = cols // SEC
    r = lax.axis_index("row")
    c = lax.axis_index("col")
    k = lax.rem(c, 2)
    z = lax.div(c, 2)
    other = 1 - k

    loads = []
    data = (slice(BASE, BASE + rows), slice(0, cols))
    for i, (src, dst) in enumerate(
        (
            (wet_h, wet_v),
            (depth_h, depth_v),
            (bed_h, bed_v),
            (mass_h, m_pad.at[data]),
            (conduct_h, cond_v),
            (settle_h, settle_v),
        )
    ):
        loads.append(pltpu.make_async_copy(src, dst, in_sem.at[i]))
        loads[-1].start()

    core_dev = (r, 2 * z + other)
    row_devs = [(lax.rem(r + j, n_row), c) for j in range(1, n_row)]
    z_devs = [(r, 2 * lax.rem(z + j, n_z) + k) for j in range(1, n_z)]
    barrier = pltpu.get_barrier_semaphore()
    for dev in [core_dev] + row_devs + z_devs:
        pl.semaphore_signal(barrier, inc=1, device_id=dev, device_id_type=MESH)
    cross = c + 2 * k - 1
    has_cross = jnp.logical_and(cross >= 0, cross < n_col)

    @pl.when(has_cross)
    def _():
        pl.semaphore_signal(barrier, inc=1, device_id=(r, cross), device_id_type=MESH)

    block = block_ref[...]
    reach = reach_ref[...]
    coef = coef_ref[...]
    n_links = block.shape[1]
    chi, clo = split(coef)
    chi, clo = chi.astype(F32), clo.astype(F32)
    spot = lax.rem(block, nblk) * rows + lax.div(block, nblk)
    for b in range(nblk):
        ids = lax.broadcasted_iota(jnp.int32, (rows, n_links), 0) + b * rows
        hot_b[b * rows : (b + 1) * rows, :] = jnp.where(ids == spot, 1.0, 0.0).astype(BF16)
    for kk in range(2):
        ids = lax.broadcasted_iota(jnp.int32, (half, n_links), 0) + kk * half
        hit = ids == reach
        hot_l[0, kk * half : (kk + 1) * half, :] = jnp.where(hit, chi, 0.0).astype(BF16)
        hot_l[1, kk * half : (kk + 1) * half, :] = jnp.where(hit, clo, 0.0).astype(BF16)

    for kk in range(2):
        for b in range(nblk):
            here = hot_b[b * rows : (b + 1) * rows, :]
            m = dot_nt(hot_l[0, kk * half : (kk + 1) * half, :], here)
            m = m + dot_nt(hot_l[1, kk * half : (kk + 1) * half, :], here)
            hi, lo = split(m)
            mat_hi[kk, :, b * rows : (b + 1) * rows] = hi
            mat_lo[kk, :, b * rows : (b + 1) * rows] = lo

    for i in range(5):
        loads[i].wait()

    @pl.loop(0, rows // CHUNK)
    def _(i):
        at = pl.ds(pl.multiple_of(i * CHUNK, CHUNK), CHUNK)
        pad = pl.ds(pl.multiple_of(BASE + i * CHUNK, 8), CHUNK)
        o = wet_v[at, :].astype(F32)
        o_pad[pad, 0:cols] = o
        c_pad[pad, 0:cols] = (0.5 * cond_v[at, :]) * o
        s_pad[pad, 0:cols] = depth_v[at, :] + bed_v[at, :]
        for b in range(nblk):
            dst = pl.ds(pl.multiple_of(b * rows + i * CHUNK, CHUNK), CHUNK)
            dcat[0, dst, 0:SEC] = o[:, b * SEC : (b + 1) * SEC].astype(BF16)

    pads = (s_pad, m_pad, c_pad, o_pad)
    lane = lax.broadcasted_iota(jnp.int32, (rows, SEC), 1)
    packed = jnp.zeros((rows, SEC), F32)
    for j, ref in enumerate(pads):
        row_send[j : j + 1, :] = ref[BASE + rows - 1 : BASE + rows, 0:cols]
        row_send[4 + j : 5 + j, :] = ref[BASE : BASE + 1, 0:cols]
        packed = jnp.where(lane == j, ref[BASE : BASE + rows, cols - 1 : cols], packed)
        packed = jnp.where(lane == 4 + j, ref[BASE : BASE + rows, 0:1], packed)
    col_send[...] = packed.T[0:8, :]

    peers = 1 + len(row_devs) + len(z_devs)
    pl.semaphore_wait(barrier, jnp.where(has_cross, peers + 1, peers))

    def remote(src, dst, ssem, rsem, dev):
        return pltpu.make_async_remote_copy(
            src_ref=src, dst_ref=dst, send_sem=ssem, recv_sem=rsem, device_id=dev, device_id_type=MESH
        )

    halo = [
        (r + 1 < n_row, r > 0, remote(row_send, row_recv.at[0], halo_s.at[0], halo_r.at[0], (lax.rem(r + 1, n_row), c)), row_recv, 0),
        (r > 0, r + 1 < n_row, remote(row_send, row_recv.at[1], halo_s.at[1], halo_r.at[1], (lax.rem(r + n_row - 1, n_row), c)), row_recv, 1),
        (c + 1 < n_col, c > 0, remote(col_send, col_recv.at[0], halo_s.at[2], halo_r.at[2], (r, lax.rem(c + 1, n_col))), col_recv, 0),
        (c > 0, c + 1 < n_col, remote(col_send, col_recv.at[1], halo_s.at[3], halo_r.at[3], (r, lax.rem(c + n_col - 1, n_col))), col_recv, 1),
    ]
    for sends, gets, copy, buf, slot in halo:
        pl.when(sends)(copy.start)

        @pl.when(jnp.logical_not(gets))
        def _():
            buf[slot] = jnp.zeros(buf.shape[1:], F32)

    core_copy = [
        remote(part.at[p, other], r_core.at[p], core_s.at[p], core_r.at[p], core_dev) for p in range(3)
    ]
    row_copy = [
        [
            remote(q_row.at[p, dev[0]], r_row.at[p, j], row_s.at[p, j], row_r.at[p, j], dev)
            for j, dev in enumerate(row_devs)
        ]
        for p in range(3)
    ]
    z_copy = [
        [
            remote(s_z.at[p, lax.div(dev[1], 2)], r_z.at[p, j], z_s.at[p, j], z_r.at[p, j], dev)
            for j, dev in enumerate(z_devs)
        ]
        for p in range(3)
    ]

    def product(p, kk):
        if p == 0:
            d = dcat[0, :, 0:SEC]
            return dot_nn(mat_hi[kk], d) + dot_nn(mat_lo[kk], d)
        both = dot_nn(mat_hi[kk], dcat[p])
        return both[:, 0:SEC] + both[:, SEC:] + dot_nn(mat_lo[kk], dcat[p, :, 0:SEC])

    def stage_core(p):
        part[p, other] = product(p, other)
        core_copy[p].start()
        part[p, k] = product(p, k)

    def stage_row(p):
        core_copy[p].wait_recv()
        q_row[p] = (part[p, k] + r_core[p]).reshape(q_row.shape[1:])
        for copy in row_copy[p]:
            copy.start()

    def stage_z(p):
        total = q_row[p, r]
        for j, copy in enumerate(row_copy[p]):
            copy.wait_recv()
            total = total + r_row[p, j]
        s_z[p] = total.reshape(s_z.shape[1:])
        for copy in z_copy[p]:
            copy.start()

    def stage_sum(p):
        total = s_z[p, z]
        for j, copy in enumerate(z_copy[p]):
            copy.wait_recv()
            total = total + r_z[p, j]
        return total

    stage_core(0)

    for kk in range(2):
        for b in range(nblk):
            here = hot_b[b * rows : (b + 1) * rows, :]
            m = dot_nt(here, hot_l[0, kk * half : (kk + 1) * half, :])
            m = m + dot_nt(here, hot_l[1, kk * half : (kk + 1) * half, :])
            hi, lo = split(m)
            mt_hi[b * rows : (b + 1) * rows, kk * half : (kk + 1) * half] = hi
            mt_lo[b * rows : (b + 1) * rows, kk * half : (kk + 1) * half] = lo
            tot = jnp.broadcast_to(jnp.sum(m, axis=1, keepdims=True), (rows, SEC))
            at = slice(b * rows, (b + 1) * rows)
            csum[at, :] = tot if kk == 0 else csum[at, :] + tot
        if kk == 0:
            stage_row(0)

    loads[5].wait()
    for sends, gets, copy, buf, slot in halo:
        pl.when(gets)(copy.wait_recv)
    for j, ref in enumerate(pads):
        ref[BASE - 1 : BASE, 0:cols] = row_recv[0, j : j + 1, :]
        ref[BASE + rows : BASE + rows + 1, 0:cols] = row_recv[1, 4 + j : 5 + j, :]
    west = jnp.concatenate([col_recv[0], jnp.zeros((SEC - 8, rows), F32)], axis=0).T
    east = jnp.concatenate([col_recv[1], jnp.zeros((SEC - 8, rows), F32)], axis=0).T
    for j, ref in enumerate(pads):
        ref[BASE : BASE + rows, cols : cols + SEC] = jnp.where(
            lane == SEC - 1, west[:, j : j + 1], east[:, 4 + j : 5 + j]
        )

    wide = cols + SEC
    for y in range(0, rows, CHUNK):
        at = pl.ds(y, CHUNK)
        pad = pl.ds(y + BASE, CHUNK)
        up = pl.ds(y + BASE - 1, CHUNK)
        down = pl.ds(y + BASE + 1, CHUNK)
        s, m, co, o = (ref[pad, :] for ref in pads)

        def roll_left(v):
            return pltpu.roll(v, wide - 1, 1)

        o2 = roll_left(o)
        a = co * o2 + roll_left(co) * o
        fw = a * (roll_left(s) - s)
        fm = a * (roll_left(m) - m)
        gw = (fw - pltpu.roll(fw, 1, 1))[:, 0:cols]
        gm = (fm - pltpu.roll(fm, 1, 1))[:, 0:cols]
        s, m, co, o = (v[:, 0:cols] for v in (s, m, co, o))
        for side in (up, down):
            a = co * o_pad[side, 0:cols] + c_pad[side, 0:cols] * o
            gw = gw + a * (s_pad[side, 0:cols] - s)
            gm = gm + a * (m_pad[side, 0:cols] - m)
        d1[at, :] = depth_v[at, :] + gw
        surf = s + gw
        s1[at, :] = surf
        mm = (m + gm) * jnp.exp(-settle_v[at, :])
        m1[at, :] = mm
        for p, v in ((1, o * surf), (2, o * mm)):
            hi, lo = split(v)
            for b in range(nblk):
                dst = pl.ds(b * rows + y, CHUNK)
                dcat[p, dst, 0:SEC] = hi[:, b * SEC : (b + 1) * SEC]
                dcat[p, dst, SEC : 2 * SEC] = lo[:, b * SEC : (b + 1) * SEC]

    stage_core(1)
    stage_z(0)
    stage_core(2)
    stage_row(1)
    stage_row(2)
    area = area_ref[...]
    rcp = 1.0 / (area + stage_sum(0))
    stage_z(1)
    stage_z(2)

    gz = [
        [
            remote(table.at[t, k, r, z], table.at[t, k, r, z], gz_s.at[t, j], gz_r.at[t, j], dev)
            for j, dev in enumerate(z_devs)
        ]
        for t in range(2)
    ]
    gr = [
        [
            remote(table.at[t, k, r], table.at[t, k, r], gr_s.at[t, j], gr_r.at[t, j], dev)
            for j, dev in enumerate(row_devs)
        ]
        for t in range(2)
    ]
    gc = [
        [
            remote(
                table.at[t, k, lax.rem(r + n_row - j, n_row)],
                table.at[t, k, lax.rem(r + n_row - j, n_row)],
                gc_s.at[t, j],
                gc_r.at[t, j],
                core_dev,
            )
            for j in range(n_row)
        ]
        for t in range(2)
    ]

    for t, (chan, out) in enumerate(((phase_ref, phase_out), (conc_ref, conc_out))):
        new = smooth((area * chan[...] + stage_sum(t + 1)) * rcp)
        out[...] = new
        table[t, k, r, z] = new
        for copy in gz[t]:
            copy.start()
    for t in range(2):
        for copy in gz[t]:
            copy.wait_recv()
        for copy in gr[t]:
            copy.start()
        gc[t][0].start()
    for t in range(2):
        for j in range(1, n_row):
            gr[t][j - 1].wait_recv()
            gc[t][j].start()
    stores = []
    for t, (src, base, ref, out) in enumerate(((s1, d1, d1, depth_out), (m1, m1, m1, mass_out))):
        for copy in gc[t]:
            copy.wait_recv()
        hi, lo = split(table[t].reshape(2 * half, SEC))
        both = jnp.concatenate([hi, lo], axis=1)
        for b in range(nblk):
            at = slice(b * rows, (b + 1) * rows)
            x = slice(b * SEC, (b + 1) * SEC)
            g = dot_nn(mt_hi[at, :], both)
            g = g[:, 0:SEC] + g[:, SEC:] + dot_nn(mt_lo[at, :], hi)
            o = o_pad[BASE : BASE + rows, x]
            ref[:, x] = base[:, x] + 0.5 * o * (g - csum[at, :] * src[:, x])
        stores.append(pltpu.make_async_copy(ref, out, out_sem.at[t]))
        stores[-1].start()

    for copy in stores:
        copy.wait()
    for sends, gets, copy, buf, slot in halo:
        pl.when(sends)(copy.wait_send)
    for p in range(3):
        core_copy[p].wait_send()
        for copy in row_copy[p] + z_copy[p]:
            copy.wait_send()
    for t in range(2):
        for copy in gz[t] + gr[t] + gc[t]:
            copy.wait_send()


def body(n_row, n_col, *args):
    depth, bed, mass, conduct, settle, wet, block, owner, reach, coef, phase, conc, area = args
    rows, cols = depth.shape
    n_links = block.shape[0]
    reach_dev = phase.shape[0]
    n_z = n_col // 2
    cells = rows * cols // SEC
    total = n_row * n_col * reach_dev
    half = total // 2
    target = owner[:, 0]
    line = target % n_col
    place = (((line % 2) * n_row + target // n_col) * n_z + line // 2) * reach_dev + reach
    row = (1, n_links)
    vm = pl.BlockSpec(memory_space=pltpu.VMEM)
    hbm = pl.BlockSpec(memory_space=pl.ANY)
    dma = pltpu.SemaphoreType.DMA
    tile = pltpu.VMEM((rows, cols), F32)
    pad = pltpu.VMEM((rows + 2 * BASE, cols + SEC), F32)
    like = lambda a: jax.ShapeDtypeStruct(a.shape, F32)
    return pl.pallas_call(
        functools.partial(kernel, n_row, n_col),
        out_shape=(like(depth), like(mass), like(phase), like(conc)),
        in_specs=[hbm] * 6 + [vm] * 6,
        out_specs=(hbm, hbm, vm, vm),
        scratch_shapes=[
            tile,
            tile,
            tile,
            tile,
            pltpu.VMEM((rows, cols), jnp.int32),
            pad,
            pad,
            pad,
            pad,
            tile,
            tile,
            tile,
            pltpu.VMEM((3, cells, 2 * SEC), BF16),
            pltpu.VMEM((2, total, n_links), BF16),
            pltpu.VMEM((cells, n_links), BF16),
            pltpu.VMEM((2, half, cells), BF16),
            pltpu.VMEM((2, half, cells), BF16),
            pltpu.VMEM((cells, total), BF16),
            pltpu.VMEM((cells, total), BF16),
            pltpu.VMEM((cells, SEC), F32),
            pltpu.VMEM((3, 2, half, SEC), F32),
            pltpu.VMEM((3, half, SEC), F32),
            pltpu.VMEM((3, n_row, half // n_row, SEC), F32),
            pltpu.VMEM((3, n_row - 1, half // n_row, SEC), F32),
            pltpu.VMEM((3, n_z, reach_dev, SEC), F32),
            pltpu.VMEM((3, n_z - 1, reach_dev, SEC), F32),
            pltpu.VMEM((2, 2, n_row, n_z, reach_dev, SEC), F32),
            pltpu.VMEM((8, cols), F32),
            pltpu.VMEM((2, 8, cols), F32),
            pltpu.VMEM((8, rows), F32),
            pltpu.VMEM((2, 8, rows), F32),
            dma((6,)),
            dma((2,)),
            dma((4,)),
            dma((4,)),
            dma((3,)),
            dma((3,)),
            dma((3, n_row - 1)),
            dma((3, n_row - 1)),
            dma((3, n_z - 1)),
            dma((3, n_z - 1)),
            dma((2, n_z - 1)),
            dma((2, n_z - 1)),
            dma((2, n_row - 1)),
            dma((2, n_row - 1)),
            dma((2, n_row)),
            dma((2, n_row)),
        ],
        compiler_params=pltpu.CompilerParams(
            collective_id=0, has_side_effects=True, vmem_limit_bytes=56 * 2**20
        ),
    )(
        depth,
        bed,
        mass,
        conduct,
        settle,
        wet,
        block.reshape(row),
        place.reshape(row),
        coef.reshape(row),
        phase,
        conc,
        area,
    )


def solution(mesh):
    both = P(("row", "col"))
    return jax.shard_map(
        functools.partial(body, mesh.shape["row"], mesh.shape["col"]),
        mesh=mesh,
        in_specs=(P("row", "col"),) * 6 + (both,) * 7,
        out_specs=(P("row", "col"), P("row", "col"), both, both),
        check_vma=False,
    )
```

```python
import functools

import jax
import jax.numpy as jnp
from jax import lax
from jax.experimental import pallas as pl
from jax.experimental.pallas import tpu as pltpu
from jax.sharding import PartitionSpec as P

MESH = pl.DeviceIdType.MESH
F32 = jnp.float32
BF16 = jnp.bfloat16
SEC = 128
BASE = 8
CHUNK = 16
PIECES = 4


def split(x):
    hi = x.astype(BF16)
    return hi, (x - hi.astype(F32)).astype(BF16)


def dot_nt(a, b):
    return lax.dot_general(a, b, (((1,), (1,)), ((), ())), preferred_element_type=F32)


def dot_nn(a, b):
    return jnp.dot(a, b, preferred_element_type=F32)


def smooth(v):
    lane = lax.broadcasted_iota(jnp.int32, v.shape, 1)
    left = jnp.where(lane == 0, v, pltpu.roll(v, 1, 1))
    right = jnp.where(lane == SEC - 1, v, pltpu.roll(v, SEC - 1, 1))
    return v + 0.25 * (left - 2.0 * v + right)


def kernel(
    n_row,
    n_col,
    depth_h,
    bed_h,
    mass_h,
    conduct_h,
    settle_h,
    wet_h,
    block_ref,
    owner_ref,
    reach_ref,
    coef_ref,
    phase_ref,
    conc_ref,
    area_ref,
    depth_out,
    mass_out,
    phase_out,
    conc_out,
    depth_v,
    bed_v,
    cond_v,
    settle_v,
    wet_v,
    s_pad,
    m_pad,
    c_pad,
    o_pad,
    d1,
    m1,
    s1,
    dcat,
    hot_l,
    hot_b,
    mat_hi,
    mat_lo,
    mt_hi,
    mt_lo,
    csum,
    part,
    r_core,
    q_row,
    r_row,
    s_z,
    r_z,
    table,
    row_send,
    row_recv,
    col_send,
    col_recv,
    in_sem,
    out_sem,
    halo_s,
    halo_r,
    core_s,
    core_r,
    row_s,
    row_r,
    z_s,
    z_r,
    gz_s,
    gz_r,
    gr_s,
    gr_r,
    gc_s,
    gc_r,
):
    rows, cols = depth_v.shape
    n_z = n_col // 2
    half = part.shape[2]
    nblk = cols // SEC
    r = lax.axis_index("row")
    c = lax.axis_index("col")
    k = lax.rem(c, 2)
    z = lax.div(c, 2)
    other = 1 - k

    loads = []
    data = (slice(BASE, BASE + rows), slice(0, cols))
    for i, (src, dst) in enumerate(
        (
            (wet_h, wet_v),
            (depth_h, depth_v),
            (bed_h, bed_v),
            (mass_h, m_pad.at[data]),
            (conduct_h, cond_v),
            (settle_h, settle_v),
        )
    ):
        loads.append(pltpu.make_async_copy(src, dst, in_sem.at[i]))
        loads[-1].start()

    core_dev = (r, 2 * z + other)
    row_devs = [(lax.rem(r + j, n_row), c) for j in range(1, n_row)]
    z_devs = [(r, 2 * lax.rem(z + j, n_z) + k) for j in range(1, n_z)]
    barrier = pltpu.get_barrier_semaphore()
    for dev in [core_dev] + row_devs + z_devs:
        pl.semaphore_signal(barrier, inc=1, device_id=dev, device_id_type=MESH)
    cross = c + 2 * k - 1
    has_cross = jnp.logical_and(cross >= 0, cross < n_col)

    @pl.when(has_cross)
    def _():
        pl.semaphore_signal(barrier, inc=1, device_id=(r, cross), device_id_type=MESH)

    block = block_ref[...]
    target = owner_ref[...]
    line = lax.rem(target, n_col)
    reach = (lax.rem(line, 2) * n_row + lax.div(target, n_col)) * n_z + lax.div(line, 2)
    reach = reach * phase_ref.shape[0] + reach_ref[...]
    coef = coef_ref[...]
    n_links = block.shape[1]
    chi, clo = split(coef)
    chi, clo = chi.astype(F32), clo.astype(F32)
    spot = lax.rem(block, nblk) * rows + lax.div(block, nblk)
    for b in range(nblk):
        ids = lax.broadcasted_iota(jnp.int32, (rows, n_links), 0) + b * rows
        hot_b[b * rows : (b + 1) * rows, :] = jnp.where(ids == spot, 1.0, 0.0).astype(BF16)
    for kk in range(2):
        ids = lax.broadcasted_iota(jnp.int32, (half, n_links), 0) + kk * half
        hit = ids == reach
        hot_l[0, kk * half : (kk + 1) * half, :] = jnp.where(hit, chi, 0.0).astype(BF16)
        hot_l[1, kk * half : (kk + 1) * half, :] = jnp.where(hit, clo, 0.0).astype(BF16)

    for kk in range(2):
        for b in range(nblk):
            here = hot_b[b * rows : (b + 1) * rows, :]
            m = dot_nt(hot_l[0, kk * half : (kk + 1) * half, :], here)
            m = m + dot_nt(hot_l[1, kk * half : (kk + 1) * half, :], here)
            hi, lo = split(m)
            mat_hi[kk, :, b * rows : (b + 1) * rows] = hi
            mat_lo[kk, :, b * rows : (b + 1) * rows] = lo

    for i in range(5):
        loads[i].wait()

    @pl.loop(0, rows // CHUNK)
    def _(i):
        at = pl.ds(pl.multiple_of(i * CHUNK, CHUNK), CHUNK)
        pad = pl.ds(pl.multiple_of(BASE + i * CHUNK, 8), CHUNK)
        o = wet_v[at, :].astype(F32)
        o_pad[pad, 0:cols] = o
        c_pad[pad, 0:cols] = (0.5 * cond_v[at, :]) * o
        s_pad[pad, 0:cols] = depth_v[at, :] + bed_v[at, :]
        for b in range(nblk):
            dst = pl.ds(pl.multiple_of(b * rows + i * CHUNK, CHUNK), CHUNK)
            dcat[0, dst, 0:SEC] = o[:, b * SEC : (b + 1) * SEC].astype(BF16)

    pads = (s_pad, m_pad, c_pad, o_pad)
    lane = lax.broadcasted_iota(jnp.int32, (rows, SEC), 1)
    packed = jnp.zeros((rows, SEC), F32)
    for j, ref in enumerate(pads):
        row_send[j : j + 1, :] = ref[BASE + rows - 1 : BASE + rows, 0:cols]
        row_send[4 + j : 5 + j, :] = ref[BASE : BASE + 1, 0:cols]
        packed = jnp.where(lane == j, ref[BASE : BASE + rows, cols - 1 : cols], packed)
        packed = jnp.where(lane == 4 + j, ref[BASE : BASE + rows, 0:1], packed)
    col_send[...] = packed.T[0:8, :]

    peers = 1 + len(row_devs) + len(z_devs)
    pl.semaphore_wait(barrier, jnp.where(has_cross, peers + 1, peers))

    def remote(src, dst, ssem, rsem, dev):
        return pltpu.make_async_remote_copy(
            src_ref=src, dst_ref=dst, send_sem=ssem, recv_sem=rsem, device_id=dev, device_id_type=MESH
        )

    halo = [
        (r + 1 < n_row, r > 0, remote(row_send, row_recv.at[0], halo_s.at[0], halo_r.at[0], (lax.rem(r + 1, n_row), c)), row_recv, 0),
        (r > 0, r + 1 < n_row, remote(row_send, row_recv.at[1], halo_s.at[1], halo_r.at[1], (lax.rem(r + n_row - 1, n_row), c)), row_recv, 1),
        (c + 1 < n_col, c > 0, remote(col_send, col_recv.at[0], halo_s.at[2], halo_r.at[2], (r, lax.rem(c + 1, n_col))), col_recv, 0),
        (c > 0, c + 1 < n_col, remote(col_send, col_recv.at[1], halo_s.at[3], halo_r.at[3], (r, lax.rem(c + n_col - 1, n_col))), col_recv, 1),
    ]
    for sends, gets, copy, buf, slot in halo:
        pl.when(sends)(copy.start)

        @pl.when(jnp.logical_not(gets))
        def _():
            buf[slot] = jnp.zeros(buf.shape[1:], F32)

    core_copy = [
        remote(part.at[p, other], r_core.at[p], core_s.at[p], core_r.at[p], core_dev) for p in range(3)
    ]
    row_copy = [
        [
            remote(q_row.at[p, dev[0]], r_row.at[p, j], row_s.at[p, j], row_r.at[p, j], dev)
            for j, dev in enumerate(row_devs)
        ]
        for p in range(3)
    ]
    z_copy = [
        [
            remote(s_z.at[p, lax.div(dev[1], 2)], r_z.at[p, j], z_s.at[p, j], z_r.at[p, j], dev)
            for j, dev in enumerate(z_devs)
        ]
        for p in range(3)
    ]

    def product(p, kk):
        if p == 0:
            d = dcat[0, :, 0:SEC]
            return dot_nn(mat_hi[kk], d) + dot_nn(mat_lo[kk], d)
        both = dot_nn(mat_hi[kk], dcat[p])
        return both[:, 0:SEC] + both[:, SEC:] + dot_nn(mat_lo[kk], dcat[p, :, 0:SEC])

    def stage_core(p):
        part[p, other] = product(p, other)
        core_copy[p].start()
        part[p, k] = product(p, k)

    def stage_row(p):
        core_copy[p].wait_recv()
        q_row[p] = (part[p, k] + r_core[p]).reshape(q_row.shape[1:])
        for copy in row_copy[p]:
            copy.start()

    def stage_z(p):
        total = q_row[p, r]
        for j, copy in enumerate(row_copy[p]):
            copy.wait_recv()
            total = total + r_row[p, j]
        s_z[p] = total.reshape(s_z.shape[1:])
        for copy in z_copy[p]:
            copy.start()

    def stage_sum(p):
        total = s_z[p, z]
        for j, copy in enumerate(z_copy[p]):
            copy.wait_recv()
            total = total + r_z[p, j]
        return total

    stage_core(0)

    for kk in range(2):
        for b in range(nblk):
            here = hot_b[b * rows : (b + 1) * rows, :]
            m = dot_nt(here, hot_l[0, kk * half : (kk + 1) * half, :])
            m = m + dot_nt(here, hot_l[1, kk * half : (kk + 1) * half, :])
            hi, lo = split(m)
            mt_hi[b * rows : (b + 1) * rows, kk * half : (kk + 1) * half] = hi
            mt_lo[b * rows : (b + 1) * rows, kk * half : (kk + 1) * half] = lo
            tot = jnp.broadcast_to(jnp.sum(m, axis=1, keepdims=True), (rows, SEC))
            at = slice(b * rows, (b + 1) * rows)
            csum[at, :] = tot if kk == 0 else csum[at, :] + tot
        if kk == 0:
            stage_row(0)

    loads[5].wait()
    for sends, gets, copy, buf, slot in halo:
        pl.when(gets)(copy.wait_recv)
    for j, ref in enumerate(pads):
        ref[BASE - 1 : BASE, 0:cols] = row_recv[0, j : j + 1, :]
        ref[BASE + rows : BASE + rows + 1, 0:cols] = row_recv[1, 4 + j : 5 + j, :]
    west = jnp.concatenate([col_recv[0], jnp.zeros((SEC - 8, rows), F32)], axis=0).T
    east = jnp.concatenate([col_recv[1], jnp.zeros((SEC - 8, rows), F32)], axis=0).T
    for j, ref in enumerate(pads):
        ref[BASE : BASE + rows, cols : cols + SEC] = jnp.where(
            lane == SEC - 1, west[:, j : j + 1], east[:, 4 + j : 5 + j]
        )

    wide = cols + SEC
    for y in range(0, rows, CHUNK):
        at = pl.ds(y, CHUNK)
        pad = pl.ds(y + BASE, CHUNK)
        up = pl.ds(y + BASE - 1, CHUNK)
        down = pl.ds(y + BASE + 1, CHUNK)
        s, m, co, o = (ref[pad, :] for ref in pads)

        def roll_left(v):
            return pltpu.roll(v, wide - 1, 1)

        o2 = roll_left(o)
        a = co * o2 + roll_left(co) * o
        fw = a * (roll_left(s) - s)
        fm = a * (roll_left(m) - m)
        gw = (fw - pltpu.roll(fw, 1, 1))[:, 0:cols]
        gm = (fm - pltpu.roll(fm, 1, 1))[:, 0:cols]
        s, m, co, o = (v[:, 0:cols] for v in (s, m, co, o))
        for side in (up, down):
            a = co * o_pad[side, 0:cols] + c_pad[side, 0:cols] * o
            gw = gw + a * (s_pad[side, 0:cols] - s)
            gm = gm + a * (m_pad[side, 0:cols] - m)
        d1[at, :] = depth_v[at, :] + gw
        surf = s + gw
        s1[at, :] = surf
        mm = (m + gm) * jnp.exp(-settle_v[at, :])
        m1[at, :] = mm
        for p, v in ((1, o * surf), (2, o * mm)):
            hi, lo = split(v)
            for b in range(nblk):
                dst = pl.ds(b * rows + y, CHUNK)
                dcat[p, dst, 0:SEC] = hi[:, b * SEC : (b + 1) * SEC]
                dcat[p, dst, SEC : 2 * SEC] = lo[:, b * SEC : (b + 1) * SEC]

    stage_core(1)
    stage_z(0)
    stage_core(2)
    stage_row(1)
    stage_row(2)
    area = area_ref[...]
    rcp = 1.0 / (area + stage_sum(0))
    stage_z(1)
    stage_z(2)

    gz = [
        [
            remote(table.at[t, k, r, z], table.at[t, k, r, z], gz_s.at[t, j], gz_r.at[t, j], dev)
            for j, dev in enumerate(z_devs)
        ]
        for t in range(2)
    ]
    gr = [
        [
            remote(table.at[t, k, r], table.at[t, k, r], gr_s.at[t, j], gr_r.at[t, j], dev)
            for j, dev in enumerate(row_devs)
        ]
        for t in range(2)
    ]
    gc = [
        [
            remote(
                table.at[t, k, lax.rem(r + n_row - j, n_row)],
                table.at[t, k, lax.rem(r + n_row - j, n_row)],
                gc_s.at[t, j],
                gc_r.at[t, j],
                core_dev,
            )
            for j in range(n_row)
        ]
        for t in range(2)
    ]

    for t, (chan, out) in enumerate(((phase_ref, phase_out), (conc_ref, conc_out))):
        new = smooth((area * chan[...] + stage_sum(t + 1)) * rcp)
        out[...] = new
        table[t, k, r, z] = new
        for copy in gz[t]:
            copy.start()
    for t in range(2):
        for copy in gz[t]:
            copy.wait_recv()
        for copy in gr[t]:
            copy.start()
        gc[t][0].start()
    for t in range(2):
        for j in range(1, n_row):
            gr[t][j - 1].wait_recv()
            gc[t][j].start()
    stores = []
    for t, (src, base, ref, out) in enumerate(((s1, d1, d1, depth_out), (m1, m1, m1, mass_out))):
        for copy in gc[t]:
            copy.wait_recv()
        hi, lo = split(table[t].reshape(2 * half, SEC))
        both = jnp.concatenate([hi, lo], axis=1)
        for b in range(nblk):
            at = slice(b * rows, (b + 1) * rows)
            x = slice(b * SEC, (b + 1) * SEC)
            g = dot_nn(mt_hi[at, :], both)
            g = g[:, 0:SEC] + g[:, SEC:] + dot_nn(mt_lo[at, :], hi)
            o = o_pad[BASE : BASE + rows, x]
            ref[:, x] = base[:, x] + 0.5 * o * (g - csum[at, :] * src[:, x])
        stores.append(pltpu.make_async_copy(ref, out, out_sem.at[t]))
        stores[-1].start()

    for copy in stores:
        copy.wait()
    for sends, gets, copy, buf, slot in halo:
        pl.when(sends)(copy.wait_send)
    for p in range(3):
        core_copy[p].wait_send()
        for copy in row_copy[p] + z_copy[p]:
            copy.wait_send()
    for t in range(2):
        for copy in gz[t] + gr[t] + gc[t]:
            copy.wait_send()


def hand_on(*refs):
    sems = refs[8]
    copies = []
    for i in range(4):
        rows = refs[i].shape[0]
        step = rows // PIECES if rows >= 8 * PIECES else rows
        for j, y in enumerate(range(0, rows, step)):
            at = pl.ds(y, step)
            copies.append(pltpu.make_async_copy(refs[i].at[at], refs[4 + i].at[at], sems.at[i, j]))
    for copy in copies:
        copy.start()
    for copy in copies:
        copy.wait()


def body(n_row, n_col, *args):
    depth, bed, mass, conduct, settle, wet, block, owner, reach, coef, phase, conc, area = args
    rows, cols = depth.shape
    n_links = block.shape[0]
    reach_dev = phase.shape[0]
    n_z = n_col // 2
    cells = rows * cols // SEC
    total = n_row * n_col * reach_dev
    half = total // 2
    row = (1, n_links)
    vm = pl.BlockSpec(memory_space=pltpu.VMEM)
    hbm = pl.BlockSpec(memory_space=pl.ANY)
    dma = pltpu.SemaphoreType.DMA
    tile = pltpu.VMEM((rows, cols), F32)
    pad = pltpu.VMEM((rows + 2 * BASE, cols + SEC), F32)
    like = lambda a: jax.ShapeDtypeStruct(a.shape, F32)
    made = pl.pallas_call(
        functools.partial(kernel, n_row, n_col),
        out_shape=(like(depth), like(mass), like(phase), like(conc)),
        in_specs=[hbm] * 6 + [vm] * 7,
        out_specs=(hbm, hbm, vm, vm),
        scratch_shapes=[
            tile,
            tile,
            tile,
            tile,
            pltpu.VMEM((rows, cols), jnp.int32),
            pad,
            pad,
            pad,
            pad,
            tile,
            tile,
            tile,
            pltpu.VMEM((3, cells, 2 * SEC), BF16),
            pltpu.VMEM((2, total, n_links), BF16),
            pltpu.VMEM((cells, n_links), BF16),
            pltpu.VMEM((2, half, cells), BF16),
            pltpu.VMEM((2, half, cells), BF16),
            pltpu.VMEM((cells, total), BF16),
            pltpu.VMEM((cells, total), BF16),
            pltpu.VMEM((cells, SEC), F32),
            pltpu.VMEM((3, 2, half, SEC), F32),
            pltpu.VMEM((3, half, SEC), F32),
            pltpu.VMEM((3, n_row, half // n_row, SEC), F32),
            pltpu.VMEM((3, n_row - 1, half // n_row, SEC), F32),
            pltpu.VMEM((3, n_z, reach_dev, SEC), F32),
            pltpu.VMEM((3, n_z - 1, reach_dev, SEC), F32),
            pltpu.VMEM((2, 2, n_row, n_z, reach_dev, SEC), F32),
            pltpu.VMEM((8, cols), F32),
            pltpu.VMEM((2, 8, cols), F32),
            pltpu.VMEM((8, rows), F32),
            pltpu.VMEM((2, 8, rows), F32),
            dma((6,)),
            dma((2,)),
            dma((4,)),
            dma((4,)),
            dma((3,)),
            dma((3,)),
            dma((3, n_row - 1)),
            dma((3, n_row - 1)),
            dma((3, n_z - 1)),
            dma((3, n_z - 1)),
            dma((2, n_z - 1)),
            dma((2, n_z - 1)),
            dma((2, n_row - 1)),
            dma((2, n_row - 1)),
            dma((2, n_row)),
            dma((2, n_row)),
        ],
        compiler_params=pltpu.CompilerParams(
            collective_id=0, has_side_effects=True, vmem_limit_bytes=56 * 2**20
        ),
    )(
        depth,
        bed,
        mass,
        conduct,
        settle,
        wet,
        block.reshape(row),
        owner.reshape(row),
        reach.reshape(row),
        coef.reshape(row),
        phase,
        conc,
        area,
    )
    return pl.pallas_call(
        hand_on,
        out_shape=tuple(like(a) for a in made),
        in_specs=[hbm] * 4,
        out_specs=(hbm,) * 4,
        scratch_shapes=[dma((4, PIECES))],
        compiler_params=pltpu.CompilerParams(vmem_limit_bytes=60 * 2**20),
    )(*made)


def solution(mesh):
    both = P(("row", "col"))
    return jax.shard_map(
        functools.partial(body, mesh.shape["row"], mesh.shape["col"]),
        mesh=mesh,
        in_specs=(P("row", "col"),) * 6 + (both,) * 7,
        out_specs=(P("row", "col"), P("row", "col"), both, both),
        check_vma=False,
    )
```
